32 devices in a mesh: groups: 2 (over x), ta: 4 (over y, core), xy: 4 (over z).
Axes of the slice: x: 2, y: 2, z: 4, core: 2. Of those that a mesh axis runs over, the one named last changes fastest.
Arguments:
- sources: bfloat16 [8, 4, 4, 8, 96, 256], P('groups', 'ta', 'xy'), parts along dimension 0, may hold values from -24 to 24
- coarse_links: bfloat16 [18, 4, 4, 4, 8, 96, 96], P('groups', None, 'ta', 'xy'), parts along dimension 0, may hold values from -0.119628906 to 0.119628906
Outputs:
- solution: float32 [8, 4, 4, 8, 96, 256], P('groups', 'ta', 'xy'), parts along dimension 0
The draws below stay inside these ranges and needn't reach their ends.
There are 2 independent parts, one for each index of `groups`. The reference program is written for one: setup_inputs(seed, part) draws one part's arguments, and reference() takes and returns one part's arrays. A program takes and returns all parts, laid end to end along the dimension named above; each array names one. Nothing has to cross between parts.
All inputs are finite; a program needn't handle non-finite values.
Results may differ from the reference program's by a relative error of at most 0.0019.
The reference program's roundings to bfloat16 on the way count: a program that leaves them out, or rounds other values in their place, can miss the bound.
Values may be sent and summed in bfloat16 or wider, within the bound.
No kernel may reach another device: no remote copies, remote signals or barrier semaphores. Data moves between devices by JAX's collectives and lax.ppermute only.
A program may use at most 128 MiB of HBM per device.

```python
import jax
import jax.numpy as jnp
from jax import lax

COMP = 96
RHS = 256
NY = 4
NZ = 8
DIRS = 9
ITERS = 2
NT = 4
NX = 4


def draw_sources(key, part):
    full_shape = (NY, NT, NX, NZ, COMP, RHS)
    subkeys = jax.random.split(jax.random.fold_in(key, 17), 4)
    rising = 1.5 * 3.0 ** (jnp.arange(NT, dtype=jnp.float32) / max(NT - 1, 1))
    rising = rising.reshape(1, NT, 1, 1, 1, 1)
    values = jax.random.normal(subkeys[3], full_shape, jnp.float32) * rising
    return jnp.clip(values, -24.0, 24.0).astype(jnp.bfloat16)


def shard_levels(rng, dims, cuts, smallest, high):
    def one(dim, blocks):
        heights = jax.random.uniform(jax.random.fold_in(jax.random.fold_in(rng, 6), dim), (blocks,), jnp.float32, smallest / len(cuts), high / len(cuts))
        return jnp.repeat(jnp.exp(heights), dims[dim] // blocks).reshape((-1,) + (1,) * (len(dims) - dim - 1))

    loudness = one(*cuts[0])
    for cut in cuts[1:]:
        loudness = loudness * one(*cut)
    return loudness


def noise(key, shape, width, bound, shards=(), kind=jnp.bfloat16):
    gain = shard_levels(key, shape, shards, -0.22, 0.18) if shards else 1.0
    array = jax.random.normal(key, shape, jnp.float32) * width * gain
    return jnp.minimum(jnp.maximum(array, -bound), bound).astype(kind)


def setup_inputs(seed: int = 0, part: int = 0) -> dict:
    splits = jax.random.split(jax.random.key(seed), 3)
    own_keys = jax.random.split(jax.random.fold_in(splits[2], part), 3)
    return {
        "sources": draw_sources(jax.random.fold_in(jax.random.fold_in(splits[2], part), 71), part),
        "coarse_links": noise(own_keys[1], (DIRS, NY, NT, NX, NZ, COMP, COMP), 0.02, 0.119628906, ((2, 4), (3, 4))),
    }


mass_term = 2.0
direction_moves = ((1, 1), (1, -1), (2, 1), (2, -1), (0, 1), (0, -1), (3, 1), (3, -1))

def link_product(link_field, vector, flipped):
    einsum_form = 'abcio,abcir->abcor' if flipped else 'abcoi,abcir->abcor'

    def one_plane(plane_pair):
        link_plane, values = plane_pair
        matrix = link_plane.astype(jnp.float32)
        entries = values.astype(jnp.float32)
        return jnp.einsum(einsum_form, matrix, entries, precision=lax.Precision.HIGHEST)
    return lax.map(one_plane, (link_field, vector))

def apply_forward(rounded, coarse_links):
    summed = mass_term * rounded.astype(jnp.float32) + link_product(coarse_links[0], rounded, False)
    for number in range(8):
        axis_number, sign_value = direction_moves[number]
        summed = summed + link_product(coarse_links[number + 1], jnp.roll(rounded, -sign_value, axis_number), False)
    return summed

def apply_adjoint(image_vec, coarse_links):
    summed = mass_term * image_vec.astype(jnp.float32) + link_product(coarse_links[0], image_vec, True)
    for number in range(8):
        axis_number, sign_value = direction_moves[number]
        adjoint_term = link_product(coarse_links[number + 1], image_vec, True).astype(jnp.bfloat16)
        summed = summed + jnp.roll(adjoint_term, sign_value, axis_number).astype(jnp.float32)
    return summed

def gram(left_vec, right_vec):
    left_rows = left_vec.reshape(-1, COMP, RHS)
    right_rows = right_vec.reshape(-1, COMP, RHS)
    return jnp.einsum('sir,sit->rt', left_rows, right_rows, precision=lax.Precision.HIGHEST)

def combine(vector, coefficients):
    return jnp.einsum('abcdir,rt->abcdit', vector, coefficients, precision=lax.Precision.HIGHEST)

def solve_spd(matrix, right_side):
    factor = jnp.linalg.cholesky(matrix)
    return jax.scipy.linalg.cho_solve((factor, True), right_side)

def reference(sources, coarse_links):
    residual = sources.astype(jnp.float32)
    solution = jnp.zeros_like(residual)
    search = residual
    energy = gram(residual, residual)
    for iteration in range(ITERS):
        rounded = search.astype(jnp.bfloat16)
        image_vec = apply_forward(rounded, coarse_links).astype(jnp.bfloat16)
        normal_image = apply_adjoint(image_vec, coarse_links)
        alpha_step = solve_spd(gram(search, normal_image), energy)
        solution = solution + combine(search, alpha_step)
        if iteration + 1 < ITERS:
            residual = residual - combine(normal_image, alpha_step)
            fresh_energy = gram(residual, residual)
            beta_step = solve_spd(energy, fresh_energy)
            search = residual + combine(search, beta_step)
            energy = fresh_energy
    return solution
```

```python
import jax
import jax.numpy as jnp
from jax import lax
from jax.sharding import PartitionSpec as P

ITERS = 2
MASS = 2.0
HIGHEST = lax.Precision.HIGHEST


def shift(value, axis, step):
    count = lax.axis_size(axis)
    return lax.ppermute(value, axis, [(i, (i + step) % count) for i in range(count)])


def swap(value, axis, bit):
    return lax.ppermute(value, axis, [(i, i ^ bit) for i in range(lax.axis_size(axis))])


def reduce_all(matrix):
    times, planes = lax.axis_size("ta"), lax.axis_size("xy")
    if times & (times - 1) or planes & (planes - 1) or times < 2:
        return lax.psum(matrix, ("ta", "xy"))
    half = matrix.shape[0] // 2
    upper = lax.rem(lax.axis_index("ta"), 2) == 0
    top, bottom = matrix[:half], matrix[half:]
    part = jnp.where(upper, top, bottom) + swap(jnp.where(upper, bottom, top), "ta", 1)
    bit = 2
    while bit < times:
        part = part + swap(part, "ta", bit)
        bit *= 2
    if planes <= 4:
        arrived = [shift(part, "xy", step) for step in range(1, planes)]
        index = lax.axis_index("xy")
        stacked = jnp.stack([part] + arrived)
        order = lax.rem(index - jnp.arange(planes) + planes, planes)
        part = jnp.sum(jnp.take(stacked, order, axis=0), axis=0)
    else:
        bit = 1
        while bit < planes:
            part = part + swap(part, "xy", bit)
            bit *= 2
    other = swap(part, "ta", 1)
    return jnp.concatenate([jnp.where(upper, part, other), jnp.where(upper, other, part)], axis=0)


def forward(link, vector):
    return jnp.einsum("yzoi,yzir->yzor", link, vector, preferred_element_type=jnp.float32)


def transposed(link, vector):
    return jnp.einsum("yzoi,yzor->yzir", link, vector, preferred_element_type=jnp.float32)


def apply_forward(vector, links):
    after_t, before_t = shift(vector, "ta", -1), shift(vector, "ta", 1)
    after_x, before_x = shift(vector, "xy", -1), shift(vector, "xy", 1)
    total = MASS * vector.astype(jnp.float32) + forward(links[0], vector)
    total += forward(links[5], jnp.roll(vector, -1, 0)) + forward(links[6], jnp.roll(vector, 1, 0))
    total += forward(links[7], jnp.roll(vector, -1, 1)) + forward(links[8], jnp.roll(vector, 1, 1))
    total += forward(links[1], after_t) + forward(links[2], before_t)
    return total + forward(links[3], after_x) + forward(links[4], before_x)


def apply_adjoint(image, links):
    products = [transposed(links[number], image).astype(jnp.bfloat16) for number in range(1, 9)]
    moved = [
        shift(products[2], "xy", 1),
        shift(products[3], "xy", -1),
        shift(products[0], "ta", 1),
        shift(products[1], "ta", -1),
    ]
    total = MASS * image.astype(jnp.float32) + transposed(links[0], image)
    for number, step, dim in ((4, 1, 0), (5, -1, 0), (6, 1, 1), (7, -1, 1)):
        total += jnp.roll(products[number], step, dim).astype(jnp.float32)
    for product in moved:
        total += product.astype(jnp.float32)
    return total


def gram(vector):
    rows = vector.reshape(-1, vector.shape[-1])
    if rows.dtype == jnp.bfloat16:
        return jnp.einsum("sr,st->rt", rows, rows, preferred_element_type=jnp.float32)
    return jnp.einsum("sr,st->rt", rows, rows, precision=HIGHEST)


def combine(vector, coefficients):
    return jnp.einsum("yzir,rt->yzit", vector.astype(jnp.float32), coefficients, precision=HIGHEST)


def body(sources, links):
    shape = sources.shape
    source = sources.reshape(shape[0], shape[3], shape[4], shape[5])
    links = links.reshape(links.shape[0], shape[0], shape[3], links.shape[-2], links.shape[-1])
    residual = source.astype(jnp.float32)
    energy = reduce_all(gram(source))
    energy_factor = jnp.linalg.cholesky(energy)
    first_image = apply_forward(source, links).astype(jnp.bfloat16)
    first_curvature = reduce_all(gram(first_image))
    normal_image = apply_adjoint(first_image, links)
    alpha = jax.scipy.linalg.cho_solve((jnp.linalg.cholesky(first_curvature), True), energy)
    residual = residual - combine(normal_image, alpha)
    rounded = residual.astype(jnp.bfloat16)
    fresh = reduce_all(gram(residual))
    beta = jax.scipy.linalg.cho_solve((energy_factor, True), fresh)
    search = residual + combine(source, beta)
    second_image = (apply_forward(rounded, links) + combine(first_image, beta)).astype(jnp.bfloat16)
    second_curvature = reduce_all(gram(second_image))
    second_alpha = jax.scipy.linalg.cho_solve((jnp.linalg.cholesky(second_curvature), True), fresh)
    answer = combine(source, alpha) + combine(search, second_alpha)
    return answer.reshape(shape)


def solution(mesh):
    return jax.shard_map(
        body,
        mesh=mesh,
        in_specs=(
            P("groups", "ta", "xy", None, None, None),
            P("groups", None, "ta", "xy", None, None, None),
        ),
        out_specs=P("groups", "ta", "xy", None, None, None),
        check_vma=False,
    )
```

```python
import functools

import jax
import jax.numpy as jnp
from jax import lax
from jax.experimental import pallas as pl
from jax.experimental.pallas import tpu as pltpu
from jax.sharding import PartitionSpec as P

MASS = 2.0
PIVOTS = 8
HIGHEST = lax.Precision.HIGHEST
F32, BF16 = jnp.float32, jnp.bfloat16
VMEM_BYTES = 48 * 2**20


def shift(value, axis, step):
    count = lax.axis_size(axis)
    return lax.ppermute(value, axis, [(i, (i + step) % count) for i in range(count)])


def swap(value, axis, bit):
    return lax.ppermute(value, axis, [(i, i ^ bit) for i in range(lax.axis_size(axis))])


def turn(value, axis, size, step):
    count = lax.axis_size(axis)
    return lax.ppermute(
        value, axis, [(i, i - i % size + (i % size + step) % size) for i in range(count)]
    )


def run_length():
    count = lax.axis_size("ta")
    return 4 if count % 4 == 0 else 2 if count % 2 == 0 else 1


def is_power(count):
    return count & (count - 1) == 0


def sum_bands(bands):
    size = len(bands)
    part = bands[0]
    for step in range(1, size):
        part = part + turn(bands[step], "ta", size, step)
    times, planes = lax.axis_size("ta"), lax.axis_size("xy")
    if is_power(times):
        bit = size
        while bit < times:
            part = part + swap(part, "ta", bit)
            bit *= 2
    else:
        held = part
        for step in range(size, times, size):
            part = part + shift(held, "ta", step)
    if planes <= 4 or not is_power(planes):
        held = part
        for step in range(1, planes):
            part = part + shift(held, "xy", step)
    else:
        bit = 1
        while bit < planes:
            part = part + swap(part, "xy", bit)
            bit *= 2
    return [part] + [turn(part, "ta", size, step) for step in range(1, size)]


def call(kernel, out_shape, grid, in_specs, out_specs, flops, moved, scratch=()):
    return pl.pallas_call(
        kernel,
        out_shape=out_shape,
        grid=grid,
        in_specs=in_specs,
        out_specs=out_specs,
        scratch_shapes=scratch,
        compiler_params=pltpu.CompilerParams(vmem_limit_bytes=VMEM_BYTES),
        cost_estimate=pl.CostEstimate(flops=flops, bytes_accessed=moved, transcendentals=0),
    )


def dot(left, right):
    return jnp.dot(left, right, preferred_element_type=F32)


def dot_rows(left, right):
    return lax.dot_general(left, right, (((0,), (0,)), ((), ())), preferred_element_type=F32)


def dot_full(left, right):
    return jnp.dot(left, right, precision=HIGHEST, preferred_element_type=F32)


def split(value, pieces):
    parts = []
    for _ in range(pieces):
        part = value.astype(BF16)
        parts.append(part)
        value = value - part.astype(F32)
    return parts


def plane_spec(shape, step=0):
    count = shape[0]
    return pl.BlockSpec(
        (None,) + tuple(shape[1:]), lambda y: (lax.rem(y + (count + step) % count, count), 0, 0, 0)
    )


def link_spec(links, number, step=0):
    count = links.shape[1]
    return pl.BlockSpec(
        (None, None) + tuple(links.shape[2:]),
        lambda y: (number, lax.rem(y + (count + step) % count, count), 0, 0, 0),
    )


def matrix_spec(shape):
    return pl.BlockSpec(tuple(shape), lambda y: (0, 0))


def like(vector, dtype):
    return jax.ShapeDtypeStruct(vector.shape, dtype)


def work(vector, products):
    planes, depth, comp, rhs = vector.shape
    return 2 * products * planes * depth * comp * comp * rhs


def inner_forward_kernel(here, above, below, later, earlier, own, lt, le, ya, yb, za, zb, out):
    depth = here.shape[0]
    for z in range(depth):
        value = here[z]
        total = MASS * value.astype(F32) + dot(own[z], value)
        total += dot(ya[z], above[z]) + dot(yb[z], below[z])
        total += dot(za[z], here[(z + 1) % depth]) + dot(zb[z], here[(z - 1) % depth])
        total += dot(lt[z], later[z]) + dot(le[z], earlier[z])
        out[z] = total


def inner_forward(vector, later, earlier, links):
    spec = plane_spec(vector.shape)
    return call(
        inner_forward_kernel,
        like(vector, F32),
        (vector.shape[0],),
        [spec, plane_spec(vector.shape, 1), plane_spec(vector.shape, -1), spec, spec]
        + [link_spec(links, number) for number in (0, 1, 2, 5, 6, 7, 8)],
        spec,
        work(vector, 7),
        16 * vector.size,
    )(vector, vector, vector, later, earlier, *([links] * 7))


def first_image_kernel(partial, ahead, behind, la, lb, image, moved_a, moved_b):
    for z in range(partial.shape[0]):
        total = partial[z] + dot(la[z], ahead[z]) + dot(lb[z], behind[z])
        rounded = total.astype(BF16)
        image[z] = rounded
        moved_a[z] = dot_rows(la[z], rounded).astype(BF16)
        moved_b[z] = dot_rows(lb[z], rounded).astype(BF16)


def first_image(partial, ahead, behind, links):
    spec = plane_spec(partial.shape)
    return call(
        first_image_kernel,
        [like(partial, BF16)] * 3,
        (partial.shape[0],),
        [spec] * 3 + [link_spec(links, 3), link_spec(links, 4)],
        [spec] * 3,
        work(partial, 4),
        14 * partial.size,
    )(partial, ahead, behind, links, links)


def time_products_kernel(image, la, lb, moved_a, moved_b):
    for z in range(image.shape[0]):
        moved_a[z] = dot_rows(la[z], image[z]).astype(BF16)
        moved_b[z] = dot_rows(lb[z], image[z]).astype(BF16)


def time_products(image, links):
    spec = plane_spec(image.shape)
    return call(
        time_products_kernel,
        [like(image, BF16)] * 2,
        (image.shape[0],),
        [spec, link_spec(links, 1), link_spec(links, 2)],
        [spec] * 2,
        work(image, 2),
        8 * image.size,
    )(image, links, links)


def inner_adjoint_kernel(here, above, below, own, ya, yb, za, zb, out):
    depth = here.shape[0]
    for z in range(depth):
        value = here[z]
        front, back = (z + 1) % depth, (z - 1) % depth
        total = MASS * value.astype(F32) + dot_rows(own[z], value)
        total += dot_rows(ya[z], below[z]).astype(BF16).astype(F32)
        total += dot_rows(yb[z], above[z]).astype(BF16).astype(F32)
        total += dot_rows(za[back], here[back]).astype(BF16).astype(F32)
        total += dot_rows(zb[front], here[front]).astype(BF16).astype(F32)
        out[z] = total


def inner_adjoint(image, links):
    spec = plane_spec(image.shape)
    return call(
        inner_adjoint_kernel,
        like(image, F32),
        (image.shape[0],),
        [spec, plane_spec(image.shape, 1), plane_spec(image.shape, -1)]
        + [link_spec(links, 0), link_spec(links, 5, -1), link_spec(links, 6, 1)]
        + [link_spec(links, 7), link_spec(links, 8)],
        spec,
        work(image, 5),
        14 * image.size,
    )(image, image, image, *([links] * 5))


def residual_kernel(partial, ta, tb, xa, xb, source, alpha, residual, rounded):
    normal = partial[...]
    for term in (ta, tb, xa, xb):
        normal += term[...].astype(F32)
    rows = (normal.shape[0] * normal.shape[1], normal.shape[2])
    moved = dot_full(normal.reshape(rows), alpha[...]).reshape(normal.shape)
    value = source[...].astype(F32) - moved
    residual[...] = value
    rounded[...] = value.astype(BF16)


def next_residual(partial, terms, source, alpha):
    spec = plane_spec(partial.shape)
    return call(
        residual_kernel,
        [like(partial, F32), like(partial, BF16)],
        (partial.shape[0],),
        [spec] * 6 + [matrix_spec(alpha.shape)],
        [spec] * 2,
        12 * partial.size * alpha.shape[0],
        20 * partial.size,
    )(partial, *terms, source, alpha)


def mixed_kernel(vector, coefficients, added, out):
    value = vector[...]
    rows = value.reshape(value.shape[0] * value.shape[1], value.shape[2])
    total = sum(dot(rows, part) for part in split(coefficients[...], 3))
    total = total.reshape(value.shape)
    out[...] = total if added is None else added[...] + total


def mixed(vector, coefficients, added=None):
    spec = plane_spec(vector.shape)
    kernel = mixed_kernel
    operands = (vector, coefficients)
    if added is None:
        kernel = lambda vector, coefficients, out: mixed_kernel(vector, coefficients, None, out)
    else:
        operands += (added,)
    return call(
        kernel,
        like(vector, F32),
        (vector.shape[0],),
        [spec, matrix_spec(coefficients.shape)] + [spec] * (len(operands) - 2),
        spec,
        6 * vector.size * coefficients.shape[0],
        10 * vector.size,
    )(*operands)


def answer_kernel(vector, coefficients, added, out):
    value = vector[...]
    rows = value.reshape(value.shape[0] * value.shape[1], value.shape[2])
    out[...] = added[...] + dot_full(rows, coefficients[...]).reshape(value.shape)


def answer(vector, coefficients, added):
    spec = plane_spec(vector.shape)
    return call(
        answer_kernel,
        like(vector, F32),
        (vector.shape[0],),
        [spec, matrix_spec(coefficients.shape), spec],
        spec,
        12 * vector.size * coefficients.shape[0],
        12 * vector.size,
    )(vector, coefficients, added)


def add_gram(total, rows):
    if rows.dtype == BF16:
        total[...] += dot_rows(rows, rows)
        return
    high, low = split(rows, 2)
    total[...] += dot_rows(high, high) + dot_rows(high, low) + dot_rows(low, high)


def put_bands(place, total, bands):
    height = bands[0].shape[0]
    for step, band in enumerate(bands):
        first = lax.rem(place[0] + step, len(bands)) * height
        band[...] = total[pl.ds(pl.multiple_of(first, height), height), :]


def gram_kernel(place, vector, *rest):
    *bands, total = rest

    @pl.when(pl.program_id(0) == 0)
    def _():
        total[...] = jnp.zeros_like(total)

    value = vector[...]
    add_gram(total, value.reshape(value.shape[0] * value.shape[1], value.shape[2]))

    @pl.when(pl.program_id(0) == pl.num_programs(0) - 1)
    def _():
        put_bands(place, total, bands)


def second_image_kernel(place, partial, ahead, behind, la, lb, *rest):
    *bands, total = rest

    @pl.when(pl.program_id(0) == 0)
    def _():
        total[...] = jnp.zeros_like(total)

    pieces = []
    for z in range(partial.shape[0]):
        value = partial[z] + dot(la[z], ahead[z]) + dot(lb[z], behind[z])
        pieces.append(value.astype(BF16))
    add_gram(total, jnp.concatenate(pieces, axis=0))

    @pl.when(pl.program_id(0) == pl.num_programs(0) - 1)
    def _():
        put_bands(place, total, bands)


def band_outputs(size, rhs):
    shape = jax.ShapeDtypeStruct((rhs // size, rhs), F32)
    return [shape] * size, [matrix_spec(shape.shape)] * size


SCALAR = pl.BlockSpec(memory_space=pltpu.SMEM)


def gram(vector, place, size):
    rhs = vector.shape[-1]
    shapes, specs = band_outputs(size, rhs)
    passes = 1 if vector.dtype == BF16 else 3
    bands = call(
        gram_kernel,
        shapes,
        (vector.shape[0],),
        [SCALAR, plane_spec(vector.shape)],
        specs,
        2 * passes * vector.size * rhs,
        vector.size * vector.dtype.itemsize,
        [pltpu.VMEM((rhs, rhs), F32)],
    )(place, vector)
    return sum_bands(bands)


def second_gram(partial, ahead, behind, links, place, size):
    rhs = partial.shape[-1]
    shapes, specs = band_outputs(size, rhs)
    spec = plane_spec(partial.shape)
    bands = call(
        second_image_kernel,
        shapes,
        (partial.shape[0],),
        [SCALAR] + [spec] * 3 + [link_spec(links, 3), link_spec(links, 4)],
        specs,
        work(partial, 2) + 2 * partial.size * rhs,
        12 * partial.size,
        [pltpu.VMEM((rhs, rhs), F32)],
    )(place, partial, ahead, behind, links, links)
    return sum_bands(bands)


def inverse_block(tile):
    side = tile.shape[0]
    rows_of = [tile[8 * v : 8 * v + 8] for v in range(side // 8)]
    lane = lax.broadcasted_iota(jnp.int32, (8, side), 1)
    line = lax.broadcasted_iota(jnp.int32, (8, side), 0)
    for first in range(0, side, PIVOTS):
        keep = (lane < first) | (lane >= first + PIVOTS)
        home, top = first // 8, first % 8
        own, rows = [], []
        for k in range(PIVOTS):
            row = jnp.broadcast_to(rows_of[home][top + k : top + k + 1, :], (8, side))
            own.append(
                [
                    jnp.broadcast_to(row[:, first + m : first + m + 1], (8, side))
                    for m in range(PIVOTS)
                ]
            )
            rows.append(jnp.where(keep, row, jnp.where(lane == first + k, 1.0, 0.0)))
        columns = [
            [jnp.broadcast_to(part[:, first + k : first + k + 1], (8, side)) for k in range(PIVOTS)]
            for part in rows_of
        ]
        lower = [[None] * PIVOTS for _ in range(PIVOTS)]
        pivot = []
        for k in range(PIVOTS):
            pivot.append(1.0 / own[k][k])
            for i in range(k + 1, PIVOTS):
                lower[i][k] = own[i][k] * pivot[k]
                for m in range(k + 1, i + 1):
                    own[i][m] = own[i][m] - lower[i][k] * own[m][k]
        for k in range(PIVOTS):
            for i in range(k + 1, PIVOTS):
                rows[i] = rows[i] - lower[i][k] * rows[k]
        solved = [rows[k] * pivot[k] for k in range(PIVOTS)]
        for k in range(PIVOTS - 1, -1, -1):
            for i in range(k + 1, PIVOTS):
                solved[k] = solved[k] - lower[i][k] * solved[i]
        updated = []
        for v, part in enumerate(rows_of):
            value = jnp.where(keep, part, 0.0)
            for k in range(PIVOTS):
                value = value - columns[v][k] * solved[k]
            if v == home:
                for k in range(PIVOTS):
                    value = jnp.where(line == top + k, solved[k], value)
            updated.append(value)
        rows_of = updated
    return jnp.concatenate(rows_of, axis=0)


def solve_kernel(place, *refs, size):
    matrix_bands, side_bands = refs[:size], refs[size : 2 * size]
    out, matrix, side = refs[2 * size :]
    height = matrix_bands[0].shape[0]
    for bands, whole in ((matrix_bands, matrix), (side_bands, side)):
        for step, band in enumerate(bands):
            first = lax.rem(place[0] + (size - step) % size, size) * height
            whole[pl.ds(pl.multiple_of(first, height), height), :] = band[...]
    half = matrix.shape[0] // 2
    upper = inverse_block(matrix[:half, :half])
    across = dot_full(upper, matrix[:half, half:])
    start = dot_full(upper, side[:half, :])
    corner = matrix[half:, :half]
    lower = inverse_block(matrix[half:, half:] - dot_full(corner, across))
    bottom = dot_full(lower, side[half:, :] - dot_full(corner, start))
    out[half:, :] = bottom
    out[:half, :] = start - dot_full(across, bottom)


def solve(matrix_bands, side_bands, place):
    size = len(matrix_bands)
    rhs = matrix_bands[0].shape[1]
    vmem = pl.BlockSpec(memory_space=pltpu.VMEM)
    return pl.pallas_call(
        functools.partial(solve_kernel, size=size),
        out_shape=jax.ShapeDtypeStruct((rhs, rhs), F32),
        in_specs=[SCALAR] + [vmem] * (2 * size),
        out_specs=vmem,
        scratch_shapes=[pltpu.VMEM((rhs, rhs), F32)] * 2,
        compiler_params=pltpu.CompilerParams(vmem_limit_bytes=VMEM_BYTES),
        cost_estimate=pl.CostEstimate(
            flops=600 * rhs**3, bytes_accessed=12 * rhs * rhs, transcendentals=0
        ),
    )(place, *matrix_bands, *side_bands)


def halo(vector):
    return (
        shift(vector, "xy", -1),
        shift(vector, "xy", 1),
        shift(vector, "ta", -1),
        shift(vector, "ta", 1),
    )


def body(sources, coarse_links):
    shape = sources.shape
    assert shape[1] == shape[2] == 1
    source = sources.reshape(shape[0], shape[3], shape[4], shape[5])
    links = coarse_links.reshape(coarse_links.shape[:2] + coarse_links.shape[4:])
    size = run_length()
    place = lax.rem(lax.axis_index("ta"), size).astype(jnp.int32).reshape(1)

    ahead, behind, later, earlier = halo(source)
    energy = gram(source, place, size)
    partial = inner_forward(source, later, earlier, links)
    image, moved_a, moved_b = first_image(partial, ahead, behind, links)
    from_behind, from_ahead = shift(moved_a, "xy", 1), shift(moved_b, "xy", -1)
    time_a, time_b = time_products(image, links)
    from_earlier, from_later = shift(time_a, "ta", 1), shift(time_b, "ta", -1)
    curvature = gram(image, place, size)
    adjoint = inner_adjoint(image, links)
    alpha = solve(curvature, energy, place)
    residual, rounded = next_residual(
        adjoint, (from_earlier, from_later, from_behind, from_ahead), source, alpha
    )

    ahead, behind, later, earlier = halo(rounded)
    fresh = gram(residual, place, size)
    partial = inner_forward(rounded, later, earlier, links)
    beta = solve(energy, fresh, place)
    partial = mixed(image, beta, partial)
    curvature = second_gram(partial, ahead, behind, links, place, size)
    search = mixed(source, beta, residual)
    begun = mixed(source, alpha)
    second_alpha = solve(curvature, fresh, place)
    return answer(search, second_alpha, begun).reshape(shape)


def solution(mesh):
    return jax.shard_map(
        body,
        mesh=mesh,
        in_specs=(
            P("groups", "ta", "xy", None, None, None),
            P("groups", None, "ta", "xy", None, None, None),
        ),
        out_specs=P("groups", "ta", "xy", None, None, None),
        check_vma=False,
    )
```

```python
import functools

import jax
import jax.numpy as jnp
from jax import lax
from jax.experimental import pallas as pl
from jax.experimental.pallas import tpu as pltpu
from jax.sharding import PartitionSpec as P

MASS = 2.0
PIVOTS = 8
HIGHEST = lax.Precision.HIGHEST
F32, BF16 = jnp.float32, jnp.bfloat16
VMEM_BYTES = 20 * 2**20


def shift(value, axis, step):
    count = lax.axis_size(axis)
    return lax.ppermute(value, axis, [(i, (i + step) % count) for i in range(count)])


def swap(value, axis, bit):
    return lax.ppermute(value, axis, [(i, i ^ bit) for i in range(lax.axis_size(axis))])


def turn(value, axis, size, step):
    count = lax.axis_size(axis)
    return lax.ppermute(
        value, axis, [(i, i - i % size + (i % size + step) % size) for i in range(count)]
    )


def run_length():
    count = lax.axis_size("ta")
    return 4 if count % 4 == 0 else 2 if count % 2 == 0 else 1


def is_power(count):
    return count & (count - 1) == 0


def first_stage(bands):
    part = bands[0]
    for step in range(1, len(bands)):
        part = part + turn(bands[step], "ta", len(bands), step)
    return part


def second_stage(part, size):
    times, planes = lax.axis_size("ta"), lax.axis_size("xy")
    if is_power(times):
        bit = size
        while bit < times:
            part = part + swap(part, "ta", bit)
            bit *= 2
    else:
        held = part
        for step in range(size, times, size):
            part = part + shift(held, "ta", step)
    if planes <= 4 or not is_power(planes):
        held = part
        for step in range(1, planes):
            part = part + shift(held, "xy", step)
    else:
        bit = 1
        while bit < planes:
            part = part + swap(part, "xy", bit)
            bit *= 2
    return part


def third_stage(part, size):
    return [part] + [turn(part, "ta", size, step) for step in range(1, size)]


def after(values, *earlier):
    held = lax.optimization_barrier((tuple(values), tuple(earlier)))[0]
    return held


def call(kernel, out_shape, grid, in_specs, out_specs, scratch=()):
    return pl.pallas_call(
        kernel,
        out_shape=out_shape,
        grid=grid,
        in_specs=in_specs,
        out_specs=out_specs,
        scratch_shapes=scratch,
        compiler_params=pltpu.CompilerParams(vmem_limit_bytes=VMEM_BYTES),
        cost_estimate=pl.CostEstimate(flops=1, bytes_accessed=1, transcendentals=0),
    )


def dot(left, right):
    return jnp.dot(left, right, preferred_element_type=F32)


def dot_rows(left, right):
    return lax.dot_general(left, right, (((0,), (0,)), ((), ())), preferred_element_type=F32)


def dot_full(left, right):
    return jnp.dot(left, right, precision=HIGHEST, preferred_element_type=F32)


def split(value, pieces):
    parts = []
    for _ in range(pieces):
        part = value.astype(BF16)
        parts.append(part)
        value = value - part.astype(F32)
    return parts


def plane_spec(shape, step=0):
    count = shape[0]
    return pl.BlockSpec(
        (None,) + tuple(shape[1:]), lambda y: (lax.rem(y + (count + step) % count, count), 0, 0, 0)
    )


def link_spec(links, number, step=0):
    count = links.shape[1]
    return pl.BlockSpec(
        (None, None) + tuple(links.shape[2:]),
        lambda y: (number, lax.rem(y + (count + step) % count, count), 0, 0, 0),
    )


def matrix_spec(shape):
    return pl.BlockSpec(tuple(shape), lambda y: (0, 0))


def like(vector, dtype):
    return jax.ShapeDtypeStruct(vector.shape, dtype)


def inner_forward_kernel(here, above, below, own, ya, yb, za, zb, out):
    depth = here.shape[0]
    for z in range(depth):
        value = here[z]
        total = MASS * value.astype(F32) + dot(own[z], value)
        total += dot(ya[z], above[z]) + dot(yb[z], below[z])
        total += dot(za[z], here[(z + 1) % depth]) + dot(zb[z], here[(z - 1) % depth])
        out[z] = total


def inner_forward(vector, links):
    spec = plane_spec(vector.shape)
    return call(
        inner_forward_kernel,
        like(vector, F32),
        (vector.shape[0],),
        [spec, plane_spec(vector.shape, 1), plane_spec(vector.shape, -1)]
        + [link_spec(links, number) for number in (0, 5, 6, 7, 8)],
        spec,
    )(vector, vector, vector, *([links] * 5))


def time_terms_kernel(partial, later, earlier, la, lb, *rest):
    out = rest[-1]
    depth, comp, rhs = partial.shape
    if len(rest) > 1:
        image, beta = rest[:2]
        rows = image[...].reshape(depth * comp, rhs)
        extra = sum(dot(rows, part) for part in split(beta[...], 2)).reshape(partial.shape)
    for z in range(depth):
        total = partial[z] + dot(la[z], later[z]) + dot(lb[z], earlier[z])
        out[z] = total + extra[z] if len(rest) > 1 else total


def time_terms(partial, later, earlier, links, image=None, beta=None):
    spec = plane_spec(partial.shape)
    specs = [spec] * 3 + [link_spec(links, 1), link_spec(links, 2)]
    operands = [partial, later, earlier, links, links]
    if image is not None:
        specs += [spec, matrix_spec(beta.shape)]
        operands += [image, beta]
    return call(
        time_terms_kernel, like(partial, F32), (partial.shape[0],), specs, spec
    )(*operands)


def packed(energy, curvature):
    row = lax.broadcasted_iota(jnp.int32, energy.shape, 0)
    column = lax.broadcasted_iota(jnp.int32, energy.shape, 1)
    diagonal = jnp.sum(jnp.where(row == column, curvature, 0.0), axis=0, keepdims=True)
    return jnp.where(row <= column, energy, curvature), diagonal


def unpacked(pair, diagonal):
    row = lax.broadcasted_iota(jnp.int32, pair.shape, 0)
    column = lax.broadcasted_iota(jnp.int32, pair.shape, 1)
    turned = pair.T
    energy = jnp.where(row <= column, pair, turned)
    curvature = jnp.where(row > column, pair, jnp.where(row == column, diagonal, turned))
    return energy, curvature


def first_image_kernel(place, partial, ahead, behind, energy, la, lb, lc, ld, image, *rest):
    products, bands, total = rest[:4], rest[4:-1], rest[-1]
    on_first(total)
    depth, comp, rhs = partial.shape
    for z in range(depth):
        value = partial[z] + dot(la[z], ahead[z]) + dot(lb[z], behind[z])
        image[z] = value.astype(BF16)
    for link, product in zip((la, lb, lc, ld), products):
        for z in range(depth):
            product[z] = dot_rows(link[z], image[z]).astype(BF16)
    add_planes(total, image)

    @pl.when(pl.program_id(0) == pl.num_programs(0) - 1)
    def _():
        pair, diagonal = packed(energy[...], total[...])
        total[...] = pair
        height = rhs // len(bands)
        put_bands(place, total, [band.at[pl.ds(0, height), :] for band in bands])
        for band in bands:
            band[pl.ds(height, 8), :] = jnp.broadcast_to(diagonal, (8, rhs))


def first_image(partial, ahead, behind, energy, links, place, size):
    spec, rhs = plane_spec(partial.shape), partial.shape[-1]
    shapes, specs = band_outputs(size, rhs, 8)
    outputs = call(
        first_image_kernel,
        [like(partial, BF16)] * 5 + shapes,
        (partial.shape[0],),
        [SCALAR] + [spec] * 3 + [matrix_spec(energy.shape)]
        + [link_spec(links, number) for number in (3, 4, 1, 2)],
        [spec] * 5 + specs,
        [pltpu.VMEM((rhs, rhs), F32)],
    )(place, partial, ahead, behind, energy, *([links] * 4))
    return outputs[0], outputs[1:5], outputs[5:]


def inner_adjoint_kernel(here, above, below, own, ya, yb, za, zb, out):
    depth = here.shape[0]
    for z in range(depth):
        value = here[z]
        front, back = (z + 1) % depth, (z - 1) % depth
        total = MASS * value.astype(F32) + dot_rows(own[z], value)
        total += dot_rows(ya[z], below[z]).astype(BF16).astype(F32)
        total += dot_rows(yb[z], above[z]).astype(BF16).astype(F32)
        total += dot_rows(za[back], here[back]).astype(BF16).astype(F32)
        total += dot_rows(zb[front], here[front]).astype(BF16).astype(F32)
        out[z] = total


def inner_adjoint(image, links):
    spec = plane_spec(image.shape)
    return call(
        inner_adjoint_kernel,
        like(image, F32),
        (image.shape[0],),
        [spec, plane_spec(image.shape, 1), plane_spec(image.shape, -1)]
        + [link_spec(links, 0), link_spec(links, 5, -1), link_spec(links, 6, 1)]
        + [link_spec(links, 7), link_spec(links, 8)],
        spec,
    )(image, image, image, *([links] * 5))


def residual_kernel(place, partial, ta, tb, xa, xb, source, alpha, residual, rounded, *rest):
    *bands, total = rest
    on_first(total)
    normal = partial[...]
    for term in (ta, tb, xa, xb):
        normal += term[...].astype(F32)
    rows = (normal.shape[0] * normal.shape[1], normal.shape[2])
    moved = dot_full(normal.reshape(rows), alpha[...]).reshape(normal.shape)
    value = source[...].astype(F32) - moved
    residual[...] = value
    rounded[...] = value.astype(BF16)
    add_planes(total, residual)
    on_last(place, total, bands)


def next_residual(partial, terms, source, alpha, place, size):
    spec, rhs = plane_spec(partial.shape), partial.shape[-1]
    shapes, specs = band_outputs(size, rhs)
    outputs = call(
        residual_kernel,
        [like(partial, F32), like(partial, BF16)] + shapes,
        (partial.shape[0],),
        [SCALAR] + [spec] * 6 + [matrix_spec(alpha.shape)],
        [spec] * 2 + specs,
        [pltpu.VMEM((rhs, rhs), F32)],
    )(place, partial, *terms, source, alpha)
    return outputs[0], outputs[1], outputs[2:]


def mixed_kernel(vector, coefficients, added, out):
    value = vector[...]
    rows = value.reshape(value.shape[0] * value.shape[1], value.shape[2])
    total = sum(dot(rows, part) for part in split(coefficients[...], 3))
    total = total.reshape(value.shape)
    out[...] = total if added is None else added[...] + total


def mixed(vector, coefficients, added=None):
    spec = plane_spec(vector.shape)
    kernel = mixed_kernel
    operands = (vector, coefficients)
    if added is None:
        kernel = lambda vector, coefficients, out: mixed_kernel(vector, coefficients, None, out)
    else:
        operands += (added,)
    return call(
        kernel,
        like(vector, F32),
        (vector.shape[0],),
        [spec, matrix_spec(coefficients.shape)] + [spec] * (len(operands) - 2),
        spec,
    )(*operands)


def answer_kernel(vector, coefficients, added, out):
    value = vector[...]
    rows = value.reshape(value.shape[0] * value.shape[1], value.shape[2])
    out[...] = added[...] + dot_full(rows, coefficients[...]).reshape(value.shape)


def answer(vector, coefficients, added):
    spec = plane_spec(vector.shape)
    return call(
        answer_kernel,
        like(vector, F32),
        (vector.shape[0],),
        [spec, matrix_spec(coefficients.shape), spec],
        spec,
    )(vector, coefficients, added)


def add_gram(total, rows):
    if rows.dtype == BF16:
        total[...] += dot_rows(rows, rows)
        return
    high, low = split(rows, 2)
    total[...] += dot_rows(high, high) + dot_rows(high, low) + dot_rows(low, high)


def put_bands(place, total, bands):
    height = bands[0].shape[0]
    for step, band in enumerate(bands):
        first = lax.rem(place[0] + step, len(bands)) * height
        band[...] = total[pl.ds(pl.multiple_of(first, height), height), :]


def on_first(total):
    @pl.when(pl.program_id(0) == 0)
    def _():
        total[...] = jnp.zeros_like(total)


def on_last(place, total, bands):
    @pl.when(pl.program_id(0) == pl.num_programs(0) - 1)
    def _():
        put_bands(place, total, bands)


def add_planes(total, vector):
    value = vector[...]
    add_gram(total, value.reshape(value.shape[0] * value.shape[1], value.shape[2]))


def gram_kernel(vector, total):
    on_first(total)
    add_planes(total, vector)


def gram(vector):
    rhs = vector.shape[-1]
    return call(
        gram_kernel,
        jax.ShapeDtypeStruct((rhs, rhs), F32),
        (vector.shape[0],),
        [plane_spec(vector.shape)],
        matrix_spec((rhs, rhs)),
    )(vector)


def second_image(partial, ahead, behind, la, lb):
    pieces = []
    for z in range(partial.shape[0]):
        value = partial[z] + dot(la[z], ahead[z]) + dot(lb[z], behind[z])
        pieces.append(value.astype(BF16))
    return jnp.concatenate(pieces, axis=0)


def second_gram_kernel(place, partial, ahead, behind, la, lb, *rest):
    *bands, total = rest
    on_first(total)
    add_gram(total, second_image(partial, ahead, behind, la, lb))
    on_last(place, total, bands)


def band_outputs(size, rhs, extra=0):
    shape = jax.ShapeDtypeStruct((rhs // size + extra, rhs), F32)
    return [shape] * size, [matrix_spec(shape.shape)] * size


SCALAR = pl.BlockSpec(memory_space=pltpu.SMEM)


def second_gram(partial, ahead, behind, links, place, size):
    rhs = partial.shape[-1]
    spec = plane_spec(partial.shape)
    shapes, out_specs = band_outputs(size, rhs)
    return call(
        second_gram_kernel,
        shapes,
        (partial.shape[0],),
        [SCALAR] + [spec] * 3 + [link_spec(links, 3), link_spec(links, 4)],
        out_specs,
        [pltpu.VMEM((rhs, rhs), F32)],
    )(place, partial, ahead, behind, links, links)


def inverse_block(tile):
    side = tile.shape[0]
    rows_of = [tile[8 * v : 8 * v + 8] for v in range(side // 8)]
    lane = lax.broadcasted_iota(jnp.int32, (8, side), 1)
    line = lax.broadcasted_iota(jnp.int32, (8, side), 0)
    for first in range(0, side, PIVOTS):
        keep = (lane < first) | (lane >= first + PIVOTS)
        home, top = first // 8, first % 8
        own, rows = [], []
        for k in range(PIVOTS):
            row = jnp.broadcast_to(rows_of[home][top + k : top + k + 1, :], (8, side))
            own.append(
                [
                    jnp.broadcast_to(row[:, first + m : first + m + 1], (8, side))
                    for m in range(PIVOTS)
                ]
            )
            rows.append(jnp.where(keep, row, jnp.where(lane == first + k, 1.0, 0.0)))
        columns = [
            [jnp.broadcast_to(part[:, first + k : first + k + 1], (8, side)) for k in range(PIVOTS)]
            for part in rows_of
        ]
        lower = [[None] * PIVOTS for _ in range(PIVOTS)]
        pivot = []
        for k in range(PIVOTS):
            pivot.append(1.0 / own[k][k])
            for i in range(k + 1, PIVOTS):
                lower[i][k] = own[i][k] * pivot[k]
                for m in range(k + 1, i + 1):
                    own[i][m] = own[i][m] - lower[i][k] * own[m][k]
        for k in range(PIVOTS):
            for i in range(k + 1, PIVOTS):
                rows[i] = rows[i] - lower[i][k] * rows[k]
        solved = [rows[k] * pivot[k] for k in range(PIVOTS)]
        for k in range(PIVOTS - 1, -1, -1):
            for i in range(k + 1, PIVOTS):
                solved[k] = solved[k] - lower[i][k] * solved[i]
        updated = []
        for v, part in enumerate(rows_of):
            value = jnp.where(keep, part, 0.0)
            for k in range(PIVOTS):
                value = value - columns[v][k] * solved[k]
            if v == home:
                for k in range(PIVOTS):
                    value = jnp.where(line == top + k, solved[k], value)
            updated.append(value)
        rows_of = updated
    return jnp.concatenate(rows_of, axis=0)


def assemble(place, bands, whole):
    size = len(bands)
    height = whole.shape[0] // size
    for step, band in enumerate(bands):
        first = lax.rem(place[0] + (size - step) % size, size) * height
        whole[pl.ds(pl.multiple_of(first, height), height), :] = band[:height, :]


def solve_into(out, matrix, side):
    half = matrix.shape[0] // 2
    upper = inverse_block(matrix[:half, :half])
    across = dot_full(upper, matrix[:half, half:])
    start = dot_full(upper, side[:half, :])
    corner = matrix[half:, :half]
    lower = inverse_block(matrix[half:, half:] - dot_full(corner, across))
    bottom = dot_full(lower, side[half:, :] - dot_full(corner, start))
    out[half:, :] = bottom
    out[:half, :] = start - dot_full(across, bottom)


def solve_both_kernel(place, *refs, size):
    bands = refs[:size]
    out, side, matrix = refs[size:]
    assemble(place, bands, side)
    height = side.shape[0] // size
    energy, curvature = unpacked(side[...], bands[0][height : height + 1, :])
    side[...] = energy
    matrix[...] = curvature
    solve_into(out, matrix, side)


def solve_side_kernel(place, matrix, *refs, size):
    out, side = refs[size:]
    assemble(place, refs[:size], side)
    solve_into(out, matrix, side)


def solve_matrix_kernel(place, side, *refs, size):
    out, matrix = refs[size:]
    assemble(place, refs[:size], matrix)
    solve_into(out, matrix, side)


def solve_call(kernel, outputs, scratch, place, operands, bands):
    rhs = bands[0].shape[1]
    vmem = pl.BlockSpec(memory_space=pltpu.VMEM)
    square = jax.ShapeDtypeStruct((rhs, rhs), F32)
    return pl.pallas_call(
        functools.partial(kernel, size=len(bands)),
        out_shape=[square] * outputs,
        in_specs=[SCALAR] + [vmem] * (len(operands) + len(bands)),
        out_specs=[vmem] * outputs,
        scratch_shapes=[pltpu.VMEM((rhs, rhs), F32)] * scratch,
        compiler_params=pltpu.CompilerParams(vmem_limit_bytes=VMEM_BYTES),
        cost_estimate=pl.CostEstimate(
            flops=1, bytes_accessed=1, transcendentals=0
        ),
    )(place, *operands, *bands)


def body(sources, coarse_links):
    shape = sources.shape
    assert shape[1] == shape[2] == 1
    source = sources.reshape(shape[0], shape[3], shape[4], shape[5])
    links = coarse_links.reshape(coarse_links.shape[:2] + coarse_links.shape[4:])
    size = run_length()
    place = lax.rem(lax.axis_index("ta"), size).astype(jnp.int32).reshape(1)

    ahead, behind = shift(source, "xy", -1), shift(source, "xy", 1)
    later, earlier = shift(source, "ta", -1), shift(source, "ta", 1)
    energy = gram(source)
    partial = time_terms(inner_forward(source, links), later, earlier, links)
    image, products, bands = first_image(partial, ahead, behind, energy, links, place, size)
    to_ahead, to_behind, to_later, to_earlier = products

    part = first_stage(bands)
    from_behind, from_earlier = shift(to_ahead, "xy", 1), shift(to_later, "ta", 1)
    part, still_image = after((part, image), part)
    adjoint = inner_adjoint(still_image, links)
    (part,) = after((part,), from_behind, from_earlier, adjoint)
    part = second_stage(part, size)
    from_ahead = shift(*after((to_behind,), part), "xy", -1)
    bands = third_stage(part, size)
    from_later = shift(*after((to_earlier,), *bands), "ta", -1)
    alpha, energy = solve_call(solve_both_kernel, 2, 1, place, (), bands)
    terms = from_earlier, from_later, from_behind, from_ahead
    residual, rounded, bands = next_residual(adjoint, terms, source, alpha, place, size)

    part = first_stage(bands)
    ahead, later = shift(rounded, "xy", -1), shift(rounded, "ta", -1)
    part, still_rounded, still_source = after((part, rounded, source), part)
    partial = inner_forward(still_rounded, links)
    begun = mixed(still_source, alpha)
    (part,) = after((part,), ahead, later, partial, begun)
    part = second_stage(part, size)
    behind = shift(*after((rounded,), part), "xy", 1)
    bands = third_stage(part, size)
    earlier = shift(*after((rounded,), *bands), "ta", 1)
    beta, fresh = solve_call(solve_side_kernel, 2, 0, place, (energy,), bands)

    partial = time_terms(partial, later, earlier, links, image, beta)
    search = mixed(source, beta, residual)
    ahead, behind = after((ahead, behind), search, begun)
    bands = second_gram(partial, ahead, behind, links, place, size)
    bands = third_stage(second_stage(first_stage(bands), size), size)
    (second_alpha,) = solve_call(solve_matrix_kernel, 1, 1, place, (fresh,), bands)
    return answer(search, second_alpha, begun).reshape(shape)


def solution(mesh):
    return jax.shard_map(
        body,
        mesh=mesh,
        in_specs=(
            P("groups", "ta", "xy", None, None, None),
            P("groups", None, "ta", "xy", None, None, None),
        ),
        out_specs=P("groups", "ta", "xy", None, None, None),
        check_vma=False,
    )
```

```python
import functools

import jax
import jax.numpy as jnp
from jax import lax
from jax.experimental import pallas as pl
from jax.experimental.pallas import tpu as pltpu
from jax.sharding import PartitionSpec as P

MASS = 2.0
PIVOTS = 8
HIGHEST = lax.Precision.HIGHEST
F32, BF16 = jnp.float32, jnp.bfloat16
VMEM_BYTES = 14 * 2**20


def shift(value, axis, step):
    count = lax.axis_size(axis)
    return lax.ppermute(value, axis, [(i, (i + step) % count) for i in range(count)])


def swap(value, axis, bit):
    return lax.ppermute(value, axis, [(i, i ^ bit) for i in range(lax.axis_size(axis))])


def turn(value, axis, size, step):
    count = lax.axis_size(axis)
    return lax.ppermute(
        value, axis, [(i, i - i % size + (i % size + step) % size) for i in range(count)]
    )


def run_length():
    count = lax.axis_size("ta")
    return 4 if count % 4 == 0 else 2 if count % 2 == 0 else 1


def is_power(count):
    return count & (count - 1) == 0


def first_stage(bands):
    part = bands[0]
    for step in range(1, len(bands)):
        part = part + turn(bands[step], "ta", len(bands), step)
    return part


def second_stage(part, size):
    times, planes = lax.axis_size("ta"), lax.axis_size("xy")
    if is_power(times):
        bit = size
        while bit < times:
            part = part + swap(part, "ta", bit)
            bit *= 2
    else:
        held = part
        for step in range(size, times, size):
            part = part + shift(held, "ta", step)
    if planes <= 4 or not is_power(planes):
        held = part
        for step in range(1, planes):
            part = part + shift(held, "xy", step)
    else:
        bit = 1
        while bit < planes:
            part = part + swap(part, "xy", bit)
            bit *= 2
    return part


def third_stage(part, size):
    return [part] + [turn(part, "ta", size, step) for step in range(1, size)]


def after(values, *earlier):
    held = lax.optimization_barrier((tuple(values), tuple(earlier)))[0]
    return held


def call(kernel, out_shape, grid, in_specs, out_specs, scratch=()):
    return pl.pallas_call(
        kernel,
        out_shape=out_shape,
        grid=grid,
        in_specs=in_specs,
        out_specs=out_specs,
        scratch_shapes=scratch,
        compiler_params=pltpu.CompilerParams(vmem_limit_bytes=VMEM_BYTES),
        cost_estimate=pl.CostEstimate(flops=1, bytes_accessed=1, transcendentals=0),
    )


def dot(left, right):
    return jnp.dot(left, right, preferred_element_type=F32)


def dot_rows(left, right):
    return lax.dot_general(left, right, (((0,), (0,)), ((), ())), preferred_element_type=F32)


def dot_full(left, right):
    return jnp.dot(left, right, precision=HIGHEST, preferred_element_type=F32)


def split(value, pieces):
    parts = []
    for _ in range(pieces):
        part = value.astype(BF16)
        parts.append(part)
        value = value - part.astype(F32)
    return parts


def plane_spec(shape, step=0):
    count = shape[0]
    return pl.BlockSpec(
        (None,) + tuple(shape[1:]), lambda y: (lax.rem(y + (count + step) % count, count), 0, 0, 0)
    )


def link_spec(links, number, step=0):
    count = links.shape[1]
    return pl.BlockSpec(
        (None, None) + tuple(links.shape[2:]),
        lambda y: (number, lax.rem(y + (count + step) % count, count), 0, 0, 0),
    )


def matrix_spec(shape):
    return pl.BlockSpec(tuple(shape), lambda y: (0, 0))


def like(vector, dtype):
    return jax.ShapeDtypeStruct(vector.shape, dtype)


def inner_forward_kernel(here, above, below, own, ya, yb, za, zb, out):
    depth = here.shape[0]
    for z in range(depth):
        value = here[z]
        total = MASS * value.astype(F32) + dot(own[z], value)
        total += dot(ya[z], above[z]) + dot(yb[z], below[z])
        total += dot(za[z], here[(z + 1) % depth]) + dot(zb[z], here[(z - 1) % depth])
        out[z] = total


def inner_forward(vector, links):
    spec = plane_spec(vector.shape)
    return call(
        inner_forward_kernel,
        like(vector, F32),
        (vector.shape[0],),
        [spec, plane_spec(vector.shape, 1), plane_spec(vector.shape, -1)]
        + [link_spec(links, number) for number in (0, 5, 6, 7, 8)],
        spec,
    )(vector, vector, vector, *([links] * 5))


def time_terms_kernel(partial, later, earlier, la, lb, out):
    for z in range(partial.shape[0]):
        out[z] = partial[z] + dot(la[z], later[z]) + dot(lb[z], earlier[z])


def time_terms(partial, later, earlier, links):
    spec = plane_spec(partial.shape)
    return call(
        time_terms_kernel,
        like(partial, F32),
        (partial.shape[0],),
        [spec] * 3 + [link_spec(links, 1), link_spec(links, 2)],
        spec,
    )(partial, later, earlier, links, links)


def joined_links_kernel(xa, xb, ta, tb, out):
    for z in range(xa.shape[0]):
        out[z] = jnp.concatenate([xa[z], xb[z], ta[z], tb[z]], axis=1)


def joined_links(links):
    shape = links.shape[1:4] + (4 * links.shape[4],)
    return call(
        joined_links_kernel,
        jax.ShapeDtypeStruct(shape, links.dtype),
        (shape[0],),
        [link_spec(links, number) for number in (3, 4, 1, 2)],
        plane_spec(shape),
    )(*([links] * 4))


def outer_terms(joined, vectors, z):
    stacked = jnp.concatenate([vector[z] for vector in vectors], axis=0)
    return dot(joined[z, :, : stacked.shape[0]], stacked)


def packed(energy, curvature):
    row = lax.broadcasted_iota(jnp.int32, energy.shape, 0)
    column = lax.broadcasted_iota(jnp.int32, energy.shape, 1)
    diagonal = jnp.sum(jnp.where(row == column, curvature, 0.0), axis=0, keepdims=True)
    return jnp.where(row <= column, energy, curvature), diagonal


def unpacked(pair, diagonal):
    row = lax.broadcasted_iota(jnp.int32, pair.shape, 0)
    column = lax.broadcasted_iota(jnp.int32, pair.shape, 1)
    turned = pair.T
    energy = jnp.where(row <= column, pair, turned)
    curvature = jnp.where(row > column, pair, jnp.where(row == column, diagonal, turned))
    return energy, curvature


def first_image_kernel(place, partial, energy, *rest):
    vectors, joined, image, products = rest[:2], rest[2], rest[3], rest[4:8]
    bands, total = rest[8:-1], rest[-1]
    on_first(total)
    depth, comp, _ = partial.shape
    for z in range(depth):
        image[z] = (partial[z] + outer_terms(joined, vectors, z)).astype(BF16)
    for z in range(depth):
        moved = dot_rows(joined[z], image[z]).astype(BF16)
        for number, product in enumerate(products):
            product[z] = moved[number * comp : (number + 1) * comp]
    add_planes(total, image)

    on_last(place, energy, total, bands)


def first_image(partial, halo, energy, joined, place, size):
    spec, rhs = plane_spec(partial.shape), partial.shape[-1]
    shapes, specs = band_outputs(size, rhs, 8)
    outputs = call(
        first_image_kernel,
        [like(partial, BF16)] * 5 + shapes,
        (partial.shape[0],),
        [SCALAR, spec, matrix_spec(energy.shape)] + [spec] * 2 + [plane_spec(joined.shape)],
        [spec] * 5 + specs,
        [pltpu.VMEM((rhs, rhs), F32)],
    )(place, partial, energy, *halo, joined)
    return outputs[0], outputs[1:5], outputs[5:]


def inner_adjoint_kernel(here, above, below, own, ya, yb, za, zb, out):
    depth = here.shape[0]
    for z in range(depth):
        value = here[z]
        front, back = (z + 1) % depth, (z - 1) % depth
        total = MASS * value.astype(F32) + dot_rows(own[z], value)
        total += dot_rows(ya[z], below[z]).astype(BF16).astype(F32)
        total += dot_rows(yb[z], above[z]).astype(BF16).astype(F32)
        total += dot_rows(za[back], here[back]).astype(BF16).astype(F32)
        total += dot_rows(zb[front], here[front]).astype(BF16).astype(F32)
        out[z] = total


def inner_adjoint(image, links):
    spec = plane_spec(image.shape)
    return call(
        inner_adjoint_kernel,
        like(image, F32),
        (image.shape[0],),
        [spec, plane_spec(image.shape, 1), plane_spec(image.shape, -1)]
        + [link_spec(links, 0), link_spec(links, 5, -1), link_spec(links, 6, 1)]
        + [link_spec(links, 7), link_spec(links, 8)],
        spec,
    )(image, image, image, *([links] * 5))


def begun_residual_kernel(partial, first, second, source, alpha, out):
    normal = partial[...] + first[...].astype(F32) + second[...].astype(F32)
    rows = (normal.shape[0] * normal.shape[1], normal.shape[2])
    moved = dot_full(normal.reshape(rows), alpha[...]).reshape(normal.shape)
    out[...] = source[...].astype(F32) - moved


def begun_residual(partial, terms, source, alpha):
    spec = plane_spec(partial.shape)
    return call(
        begun_residual_kernel,
        like(partial, F32),
        (partial.shape[0],),
        [spec] * 4 + [matrix_spec(alpha.shape)],
        spec,
    )(partial, *terms, source, alpha)


def residual_kernel(begun, first, second, alpha, residual, rounded):
    value = first[...].astype(F32) + second[...].astype(F32)
    rows = (value.shape[0] * value.shape[1], value.shape[2])
    high, low = split(value.reshape(rows), 2)
    upper, middle, lower = split(alpha[...], 3)
    moved = dot(high, upper) + (dot(high, middle) + dot(low, upper))
    moved += dot(high, lower) + dot(low, middle)
    total = begun[...] - moved.reshape(value.shape)
    residual[...] = total
    rounded[...] = total.astype(BF16)


def next_residual(begun, first, second, alpha):
    spec = plane_spec(begun.shape)
    return call(
        residual_kernel,
        [like(begun, F32), like(begun, BF16)],
        (begun.shape[0],),
        [spec] * 3 + [matrix_spec(alpha.shape)],
        [spec] * 2,
    )(begun, first, second, alpha)


def answer_kernel(source, residual, first, second, out):
    rows = (source.shape[0] * source.shape[1], source.shape[2])
    value = source[...].reshape(rows)
    total = sum(dot(value, part) for part in split(first[...], 3))
    high, low = split(residual[...].reshape(rows), 2)
    upper, lower = split(second[...], 2)
    total += dot(high, upper) + (dot(high, lower) + dot(low, upper))
    out[...] = total.reshape(source.shape)


def answer(source, residual, first, second):
    spec = plane_spec(source.shape)
    return call(
        answer_kernel,
        like(source, F32),
        (source.shape[0],),
        [spec] * 2 + [matrix_spec(first.shape)] * 2,
        spec,
    )(source, residual, first, second)


def add_gram(total, rows):
    if rows.dtype == BF16:
        total[...] += dot_rows(rows, rows)
        return
    high, low = split(rows, 2)
    total[...] += dot_rows(high, high) + dot_rows(high, low) + dot_rows(low, high)


def put_bands(place, total, bands):
    height = bands[0].shape[0]
    for step, band in enumerate(bands):
        first = lax.rem(place[0] + step, len(bands)) * height
        band[...] = total[pl.ds(pl.multiple_of(first, height), height), :]


def on_first(total):
    @pl.when(pl.program_id(0) == 0)
    def _():
        total[...] = jnp.zeros_like(total)


def on_last(place, other, total, bands):
    @pl.when(pl.program_id(0) == pl.num_programs(0) - 1)
    def _():
        pair, diagonal = packed(other[...], total[...])
        total[...] = pair
        rhs = total.shape[0]
        height = rhs // len(bands)
        put_bands(place, total, [band.at[pl.ds(0, height), :] for band in bands])
        for band in bands:
            band[pl.ds(height, 8), :] = jnp.broadcast_to(diagonal, (8, rhs))


def add_planes(total, vector):
    value = vector[...]
    add_gram(total, value.reshape(value.shape[0] * value.shape[1], value.shape[2]))


def gram_kernel(vector, total):
    on_first(total)
    add_planes(total, vector)


def gram(vector):
    rhs = vector.shape[-1]
    return call(
        gram_kernel,
        jax.ShapeDtypeStruct((rhs, rhs), F32),
        (vector.shape[0],),
        [plane_spec(vector.shape)],
        matrix_spec((rhs, rhs)),
    )(vector)


def second_image(partial, vectors, joined):
    pieces = []
    for z in range(partial.shape[0]):
        pieces.append((partial[z] + outer_terms(joined, vectors, z)).astype(BF16))
    return jnp.concatenate(pieces, axis=0)


def second_gram_kernel(place, partial, fresh, *rest):
    vectors, joined, bands, total = rest[:4], rest[4], rest[5:-1], rest[-1]
    on_first(total)
    add_gram(total, second_image(partial, vectors, joined))
    on_last(place, fresh, total, bands)


def band_outputs(size, rhs, extra):
    shape = jax.ShapeDtypeStruct((rhs // size + extra, rhs), F32)
    return [shape] * size, [matrix_spec(shape.shape)] * size


SCALAR = pl.BlockSpec(memory_space=pltpu.SMEM)


def second_gram(partial, halo, fresh, joined, place, size):
    rhs = partial.shape[-1]
    spec = plane_spec(partial.shape)
    shapes, out_specs = band_outputs(size, rhs, 8)
    return call(
        second_gram_kernel,
        shapes,
        (partial.shape[0],),
        [SCALAR, spec, matrix_spec(fresh.shape)] + [spec] * 4 + [plane_spec(joined.shape)],
        out_specs,
        [pltpu.VMEM((rhs, rhs), F32)],
    )(place, partial, fresh, *halo, joined)


def inverse_block(tile):
    side = tile.shape[0]
    rows_of = [tile[8 * v : 8 * v + 8] for v in range(side // 8)]
    lane = lax.broadcasted_iota(jnp.int32, (8, side), 1)
    line = lax.broadcasted_iota(jnp.int32, (8, side), 0)
    for first in range(0, side, PIVOTS):
        keep = (lane < first) | (lane >= first + PIVOTS)
        home, top = first // 8, first % 8
        own, rows = [], []
        for k in range(PIVOTS):
            row = jnp.broadcast_to(rows_of[home][top + k : top + k + 1, :], (8, side))
            own.append(
                [
                    jnp.broadcast_to(row[:, first + m : first + m + 1], (8, side))
                    for m in range(PIVOTS)
                ]
            )
            rows.append(jnp.where(keep, row, jnp.where(lane == first + k, 1.0, 0.0)))
        columns = [
            [jnp.broadcast_to(part[:, first + k : first + k + 1], (8, side)) for k in range(PIVOTS)]
            for part in rows_of
        ]
        lower = [[None] * PIVOTS for _ in range(PIVOTS)]
        pivot = []
        for k in range(PIVOTS):
            pivot.append(1.0 / own[k][k])
            for i in range(k + 1, PIVOTS):
                lower[i][k] = own[i][k] * pivot[k]
                for m in range(k + 1, i + 1):
                    own[i][m] = own[i][m] - lower[i][k] * own[m][k]
        for k in range(PIVOTS):
            for i in range(k + 1, PIVOTS):
                rows[i] = rows[i] - lower[i][k] * rows[k]
        solved = [rows[k] * pivot[k] for k in range(PIVOTS)]
        for k in range(PIVOTS - 1, -1, -1):
            for i in range(k + 1, PIVOTS):
                solved[k] = solved[k] - lower[i][k] * solved[i]
        updated = []
        for v, part in enumerate(rows_of):
            value = jnp.where(keep, part, 0.0)
            for k in range(PIVOTS):
                value = value - columns[v][k] * solved[k]
            if v == home:
                for k in range(PIVOTS):
                    value = jnp.where(line == top + k, solved[k], value)
            updated.append(value)
        rows_of = updated
    return jnp.concatenate(rows_of, axis=0)


def assemble(place, bands, whole):
    size = len(bands)
    height = whole.shape[0] // size
    for step, band in enumerate(bands):
        first = lax.rem(place[0] + (size - step) % size, size) * height
        whole[pl.ds(pl.multiple_of(first, height), height), :] = band[:height, :]


def solve_into(out, matrix, side):
    half = matrix.shape[0] // 2
    upper = inverse_block(matrix[:half, :half])
    across = dot_full(upper, matrix[:half, half:])
    start = dot_full(upper, side[:half, :])
    corner = matrix[half:, :half]
    lower = inverse_block(matrix[half:, half:] - dot_full(corner, across))
    bottom = dot_full(lower, side[half:, :] - dot_full(corner, start))
    out[half:, :] = bottom
    out[:half, :] = start - dot_full(across, bottom)


def unpack_bands(place, bands, scratch):
    assemble(place, bands, scratch)
    height = scratch.shape[0] // len(bands)
    return unpacked(scratch[...], bands[0][height : height + 1, :])


def first_solve_kernel(place, *refs, size):
    bands = refs[:size]
    alpha, energy, curvature = refs[size:]
    energy[...], curvature[...] = unpack_bands(place, bands, alpha)
    solve_into(alpha, curvature, energy)


def inverse_kernel(place, matrix, out, unit):
    row = lax.broadcasted_iota(jnp.int32, unit.shape, 0)
    column = lax.broadcasted_iota(jnp.int32, unit.shape, 1)
    unit[...] = jnp.where(row == column, 1.0, 0.0)
    solve_into(out, matrix, unit)


def second_solve_kernel(place, inverse, first, alpha, *refs, size):
    bands = refs[:size]
    out, weights, matrix, fresh = refs[size:]
    fresh[...], image_gram = unpack_bands(place, bands, matrix)
    beta = dot_full(inverse[...], fresh[...])
    moved = dot_full(first[...], beta)
    less = lax.dot_general(
        beta, moved, (((0,), (0,)), ((), ())), precision=HIGHEST, preferred_element_type=F32
    )
    matrix[...] = image_gram - less
    solve_into(out, matrix, fresh)
    weights[...] = alpha[...] + dot_full(beta, out[...])


def solve_call(kernel, outputs, scratch, place, *operands):
    rhs = operands[-1].shape[1]
    vmem = pl.BlockSpec(memory_space=pltpu.VMEM)
    square = jax.ShapeDtypeStruct((rhs, rhs), F32)
    return pl.pallas_call(
        kernel,
        out_shape=[square] * outputs,
        in_specs=[SCALAR] + [vmem] * len(operands),
        out_specs=[vmem] * outputs,
        scratch_shapes=[pltpu.VMEM((rhs, rhs), F32)] * scratch,
        compiler_params=pltpu.CompilerParams(vmem_limit_bytes=VMEM_BYTES),
        cost_estimate=pl.CostEstimate(flops=1, bytes_accessed=1, transcendentals=0),
    )(place, *operands)


def body(sources, coarse_links):
    shape = sources.shape
    assert shape[1] == shape[2] == 1
    source = sources.reshape(shape[0], shape[3], shape[4], shape[5])
    links = coarse_links.reshape(coarse_links.shape[:2] + coarse_links.shape[4:])
    size = run_length()
    place = lax.rem(lax.axis_index("ta"), size).astype(jnp.int32).reshape(1)

    ahead, behind = shift(source, "xy", -1), shift(source, "xy", 1)
    later, earlier = shift(source, "ta", -1), shift(source, "ta", 1)
    energy = gram(source)
    partial = inner_forward(source, links)
    (late_links,) = after((links,), later, earlier)
    partial = time_terms(partial, later, earlier, late_links)
    joined = joined_links(late_links)
    x_halo = after((ahead, behind), partial, energy, joined)
    image, products, bands = first_image(partial, x_halo, energy, joined, place, size)
    to_ahead, to_behind, to_later, to_earlier = products

    part = first_stage(bands)
    from_behind, from_earlier = shift(to_ahead, "xy", 1), shift(to_later, "ta", 1)
    part, still_image = after((part, image), part)
    adjoint = inner_adjoint(still_image, links)
    (part,) = after((part,), from_behind, from_earlier, adjoint)
    part = second_stage(part, size)
    from_ahead = shift(*after((to_behind,), part), "xy", -1)
    bands = third_stage(part, size)
    from_later = shift(*after((to_earlier,), *bands), "ta", -1)
    first_solve = functools.partial(first_solve_kernel, size=size)
    alpha, energy, curvature = solve_call(first_solve, 3, 0, place, *bands)
    begun = begun_residual(adjoint, (from_earlier, from_behind), source, alpha)
    from_ahead, from_later = after((from_ahead, from_later), begun)
    residual, rounded = next_residual(begun, from_ahead, from_later, alpha)

    ahead, behind = shift(rounded, "xy", -1), shift(rounded, "xy", 1)
    later, earlier = shift(rounded, "ta", -1), shift(rounded, "ta", 1)
    partial = inner_forward(rounded, links)
    fresh = gram(residual)
    (inverse,) = solve_call(inverse_kernel, 1, 1, place, energy)
    x_halo = after((ahead, behind), partial, fresh, inverse)
    t_halo = after((later, earlier), *x_halo)
    bands = second_gram(partial, x_halo + t_halo, fresh, joined, place, size)
    bands = third_stage(second_stage(first_stage(bands), size), size)
    second_solve = functools.partial(second_solve_kernel, size=size)
    second_alpha, weights = solve_call(
        second_solve, 2, 2, place, inverse, curvature, alpha, *bands
    )
    return answer(source, residual, weights, second_alpha).reshape(shape)


def solution(mesh):
    return jax.shard_map(
        body,
        mesh=mesh,
        in_specs=(
            P("groups", "ta", "xy", None, None, None),
            P("groups", None, "ta", "xy", None, None, None),
        ),
        out_specs=P("groups", "ta", "xy", None, None, None),
        check_vma=False,
    )
```
